32 devices in a mesh: inst: 2 (over y), ax: 8 (over z, core), circ: 2 (over x).
Axes of the slice: x: 2, y: 2, z: 4, core: 2. Of those that a mesh axis runs over, the one named last changes fastest.
Arguments:
- flow_state: float32 [2, 7, 64, 128, 128], P('inst', None, 'ax', 'circ'), may hold values from -2 to 40, as said below
- thinc_flags: int32 [2, 64, 128], P('inst', 'ax', 'circ'), may hold values 0 or 1
Outputs:
- new_state: float32 [2, 7, 64, 128, 128], P('inst', None, 'ax', 'circ')
The draws below stay inside these ranges and needn't reach their ends.
Inputs may be any that keep to these rules, and one draw needn't show every extreme that they name: `flow_state`: every cell holds a two-phase state with positive partial densities and positive pressure, whose seventh field, the volume fraction, lies between 0.02 and 0.98.
All inputs are finite; a program needn't handle non-finite values. No bound on the sum of `thinc_flags` on one device may be relied on, other than what follows from the above.
Results may differ from the reference program's by a relative error of at most 0.0003.
Values sent between devices are 32-bit elements; how exact they have to be, the bound alone decides.
A program may use at most 64 MiB of HBM per device.

```python
import jax
import jax.numpy as jnp
from jax import lax

RADIAL = 128
INSTANCES = 2
AXIAL = 64
CIRCUM = 128


G_LIQ = 4.4


P_LIQ = 6.0


G_GAS = 1.4


def draw_flow_state(key, part):
    streams = jax.random.split(jax.random.fold_in(key, 17), 8)
    grid_shape = (INSTANCES, AXIAL, CIRCUM, RADIAL)
    fraction = jax.random.uniform(streams[0], grid_shape, jnp.float32, 0.02, 0.98)
    dens_liq = jax.random.uniform(streams[1], grid_shape, jnp.float32, 0.8, 1.2)
    dens_gas = jax.random.uniform(streams[2], grid_shape, jnp.float32, 0.1, 0.3)
    pressure = jax.random.uniform(streams[3], grid_shape, jnp.float32, 0.5, 2.0)
    vel_ax = 1.0 + 0.4 * jax.random.truncated_normal(streams[4], -2.0, 2.0, grid_shape, jnp.float32)
    vel_circ = 0.4 * jax.random.truncated_normal(streams[5], -2.0, 2.0, grid_shape, jnp.float32)
    vel_rad = 0.25 * jax.random.truncated_normal(streams[6], -2.0, 2.0, grid_shape, jnp.float32)
    part_liq = fraction * dens_liq
    part_gas = (1.0 - fraction) * dens_gas
    density = part_liq + part_gas
    gamma_term = fraction / (G_LIQ - 1.0) + (1.0 - fraction) / (G_GAS - 1.0)
    stiff_term = fraction * (G_LIQ * P_LIQ / (G_LIQ - 1.0))
    kinetic = 0.5 * density * (vel_ax * vel_ax + vel_circ * vel_circ + vel_rad * vel_rad)
    energy = gamma_term * pressure + stiff_term + kinetic
    return jnp.stack([part_liq, part_gas, density * vel_ax, density * vel_circ, density * vel_rad, energy, fraction], axis=1)


def touch_ends(array, rng, smallest, high):
    index_at = [jax.random.randint(jax.random.fold_in(rng, axis), (), 0, length) for axis, length in enumerate(array.shape)]
    longest = array.shape.index(max(array.shape))
    beside = index_at[:longest] + [(index_at[longest] + 1) % array.shape[longest]] + index_at[longest + 1:]
    return array.at[tuple(index_at)].set(smallest).at[tuple(beside)].set(high)


def setup_inputs(seed: int = 0) -> dict:
    keys = jax.random.split(jax.random.key(seed), 3)
    return {
        "flow_state": draw_flow_state(jax.random.fold_in(keys[2], 71), 0),
        "thinc_flags": touch_ends((jax.random.randint(keys[1], (INSTANCES, AXIAL, CIRCUM), 0, 2) < 1).astype(jnp.int32), jax.random.fold_in(keys[1], 1), 0, 1),
    }


G_LIQ = 4.4
P_LIQ = 6.0
G_GAS = 1.4
BETA = 1.6
EPSA = 0.1
ALPHA = 4.0
DIAG0 = 0.016
OMEGA = 1.0
NU_T = 0.25

def spectral_table(period_count):
    harmonic = jnp.arange(period_count, dtype=jnp.int32)
    phase_angle = jnp.pi / period_count * harmonic.astype(jnp.float32)
    sine_safe = jnp.where(harmonic == 0, 1.0, jnp.sin(phase_angle))
    parity = jnp.where(harmonic % 2 == 0, 1.0, -1.0)
    first_der = jnp.where(harmonic == 0, 0.0, 0.5 * parity * jnp.cos(phase_angle) / sine_safe)
    second = jnp.where(harmonic == 0, -(period_count * period_count + 2) / 12.0, -parity / (2.0 * sine_safe * sine_safe))
    return OMEGA * first_der - NU_T * OMEGA * OMEGA * second

def primitives(cells):
    density = cells[0] + cells[1]
    vel_ax = cells[2] / density
    vel_circ = cells[3] / density
    vel_rad = cells[4] / density
    fraction = cells[6]
    gamma_term = fraction / (G_LIQ - 1.0) + (1.0 - fraction) / (G_GAS - 1.0)
    stiff_term = fraction * (G_LIQ * P_LIQ / (G_LIQ - 1.0))
    kinetic = 0.5 * density * (vel_ax * vel_ax + vel_circ * vel_circ + vel_rad * vel_rad)
    pressure = (cells[5] - kinetic - stiff_term) / gamma_term
    sound_speed = jnp.sqrt(((1.0 + 1.0 / gamma_term) * pressure + stiff_term / gamma_term) / density)
    return (density, vel_ax, vel_circ, pressure, sound_speed)

def sharpen(lower_val, centre, upper_val, offset):
    average = 0.5 * (lower_val + upper_val)
    difference = upper_val - lower_val
    steepness = 2.0 * (centre - average) / (jnp.abs(difference) + EPSA)
    return average + 0.5 * difference * jnp.tanh(BETA * (steepness + offset))

def physical(cells, fraction, circ_vel, pressure):
    return [cells[0] * circ_vel, cells[1] * circ_vel, cells[2] * circ_vel, cells[3] * circ_vel + pressure, cells[4] * circ_vel, (cells[5] + pressure) * circ_vel, fraction * circ_vel]

def face_flux(left_state, right_state, frac_left, frac_right):
    _, _, circ_left, press_left, sound_left = primitives(left_state)
    _, _, circ_right, press_right, sound_right = primitives(right_state)
    speed = jnp.maximum(jnp.abs(circ_left) + sound_left, jnp.abs(circ_right) + sound_right)
    flux_left = physical(left_state, frac_left, circ_left, press_left)
    flux_right = physical(right_state, frac_right, circ_right, press_right)
    jumps = [right_state[component] - left_state[component] for component in range(6)]
    jumps.append(frac_right - frac_left)
    return jnp.stack([0.5 * (flux_left[component] + flux_right[component]) - 0.5 * speed * jumps[component] for component in range(7)])

def circ_residual(cells, flag_block):
    fraction = cells[6]
    frac_back2 = jnp.roll(fraction, 2, axis=1)
    frac_back1 = jnp.roll(fraction, 1, axis=1)
    frac_next = jnp.roll(fraction, -1, axis=1)
    flagged = (flag_block > 0)[:, :, None]
    frac_left = jnp.where(flagged, sharpen(frac_back2, frac_back1, fraction, 1.0), frac_back1)
    frac_right = jnp.where(flagged, sharpen(frac_back1, fraction, frac_next, -1.0), fraction)
    fluxes = face_flux(jnp.roll(cells, 1, axis=2), cells, frac_left, frac_right)
    return jnp.roll(fluxes, -1, axis=2) - fluxes

def advance(operands):
    cells, spectral, flag_block = operands
    residual = circ_residual(cells, flag_block) + spectral
    _, vel_ax, _, _, sound_speed = primitives(cells)
    radius = jnp.abs(vel_ax) + sound_speed
    coupling = jnp.moveaxis(-ALPHA * radius, 0, -1)
    diagonal = jnp.moveaxis(DIAG0 + 2.0 * ALPHA * radius, 0, -1)
    lower_coef = coupling.at[..., 0].set(0.0)
    upper_coef = coupling.at[..., -1].set(0.0)
    full_shape = (cells.shape[0],) + coupling.shape
    right_side = jnp.moveaxis(-residual, 1, -1)[..., None]
    delta = lax.linalg.tridiagonal_solve(jnp.broadcast_to(lower_coef, full_shape), jnp.broadcast_to(diagonal, full_shape), jnp.broadcast_to(upper_coef, full_shape), right_side)[..., 0]
    return cells + jnp.moveaxis(delta, -1, 1)

def reference(flow_state, thinc_flags):
    period_count = flow_state.shape[0]
    table_values = spectral_table(period_count)
    positions = jnp.arange(period_count, dtype=jnp.int32)
    lag_index = (positions[:, None] - positions[None, :]) % period_count
    weight_matrix = table_values[lag_index]
    spectral = jnp.einsum('nm,mfacr->nfacr', weight_matrix, flow_state, precision=lax.Precision.HIGHEST)
    return lax.map(advance, (flow_state, spectral, thinc_flags))
```

```python
import functools
import math

import jax
import jax.numpy as jnp
import numpy as np
from jax import lax
from jax.experimental import pallas as pl
from jax.experimental.pallas import tpu as pltpu
from jax.sharding import PartitionSpec as P

G_LIQ = 4.4
P_LIQ = 6.0
G_GAS = 1.4
BETA = 1.6
EPSA = 0.1
ALPHA = 4.0
DIAG0 = 0.016
OMEGA = 1.0
NU_T = 0.25
MESH = pl.DeviceIdType.MESH
TILE = 8


def spectral_weights(count):
    weights = []
    for k in range(count):
        if k == 0:
            first, second = 0.0, -(count * count + 2) / 12.0
        else:
            angle = math.pi * k / count
            parity = 1.0 if k % 2 == 0 else -1.0
            first = 0.5 * parity * math.cos(angle) / math.sin(angle)
            second = -parity / (2.0 * math.sin(angle) ** 2)
        weights.append(float(np.float32(OMEGA * first - NU_T * OMEGA * OMEGA * second)))
    return weights


def sharpen(lower_val, centre, upper_val, offset):
    average = 0.5 * (lower_val + upper_val)
    difference = upper_val - lower_val
    steepness = 2.0 * (centre - average) / (jnp.abs(difference) + EPSA)
    return average + 0.5 * difference * jnp.tanh(BETA * (steepness + offset))


def primitives(q):
    density = q[0] + q[1]
    inv = 1.0 / density
    vel_ax = q[2] * inv
    vel_circ = q[3] * inv
    vel_rad = q[4] * inv
    fraction = q[6]
    gamma_term = fraction / (G_LIQ - 1.0) + (1.0 - fraction) / (G_GAS - 1.0)
    stiff_term = fraction * (G_LIQ * P_LIQ / (G_LIQ - 1.0))
    kinetic = 0.5 * (vel_ax * q[2] + vel_circ * q[3] + vel_rad * q[4])
    inv_gamma = 1.0 / gamma_term
    pressure = (q[5] - kinetic - stiff_term) * inv_gamma
    sound = jnp.sqrt((pressure + (pressure + stiff_term) * inv_gamma) * inv)
    return vel_ax, vel_circ, pressure, sound


def kernel(sizes, weights, q_hbm, flag_ref, out_hbm, pad, prim, flux, bg, iv, piv, phi, psi, rem,
           halo_out, halo_in, chain_out, chain_in, coef, ps, zrecv, ag_out, ag_in,
           load_sem, ysend, yrecv, hsend, hrecv, csend, crecv, zsend, zrecv_sem, fsend, frecv, osem):
    n_inst, n_ax, n_circ, rows, width, radial = sizes
    fields = 7
    chunks = width // TILE
    block = 4 if rows % 4 == 0 else 1
    i, me, c = lax.axis_index("inst"), lax.axis_index("ax"), lax.axis_index("circ")
    core = lax.rem(me, 2)
    base = me - core
    sibling = base + 1 - core
    above, below = lax.rem(c + 1, n_circ), lax.rem(c + n_circ - 1, n_circ)

    def tile(j):
        return pl.ds(pl.multiple_of(j * TILE, TILE), TILE)

    load = pltpu.make_async_copy(q_hbm.at[0], pad.at[:, :, pl.ds(TILE, width), :], load_sem)
    load.start()

    barrier = pltpu.get_barrier_semaphore()
    for k in range(1, n_inst):
        pl.semaphore_signal(barrier, inc=1, device_id=(lax.rem(i + k, n_inst), me, c), device_id_type=MESH)
    for k in range(1, n_ax):
        pl.semaphore_signal(barrier, inc=1, device_id=(i, lax.rem(me + k, n_ax), c), device_id_type=MESH)
    for other in (above, below):
        pl.semaphore_signal(barrier, inc=1, device_id=(i, me, other), device_id_type=MESH)
    pl.semaphore_wait(barrier, n_inst + n_ax)

    def ycopy(k, j):
        return pltpu.make_async_remote_copy(
            src_ref=q_hbm.at[0, :, :, tile(j), :], dst_ref=rem.at[k - 1, :, :, tile(j), :],
            send_sem=ysend.at[k - 1, j], recv_sem=yrecv.at[k - 1, j],
            device_id=(lax.rem(i + k, n_inst), me, c), device_id_type=MESH)

    for j in range(chunks):
        for k in range(1, n_inst):
            ycopy(k, j).start()

    load.wait()

    for f in range(fields):
        halo_out[0, f] = pad[f, :, TILE + width - 1, :]
        halo_out[1, f] = pad[f, :, TILE, :]
    halo_out[0, fields] = pad[fields - 1, :, TILE + width - 2, :]
    halo_out[1, fields] = pad[fields - 1, :, TILE + 1, :]
    halo_out[0, fields + 1] = flag_ref[:, 0, :]
    halo_out[1, fields + 1] = flag_ref[:, 0, :]
    halos = [
        pltpu.make_async_remote_copy(
            src_ref=halo_out.at[side], dst_ref=halo_in.at[side], send_sem=hsend.at[side],
            recv_sem=hrecv.at[side], device_id=(i, me, (above, below)[side]), device_id_type=MESH)
        for side in range(2)
    ]
    for copy in halos:
        copy.start()

    def own_tile(j, carry):
        at = tile(j + 1)
        here = tile(j)
        for a0 in range(0, rows, block):
            part = pl.ds(a0, block)
            vel_ax, vel_circ, pressure, sound = primitives([pad[f, part, at, :] for f in range(fields)])
            prim[0, part, at, :] = vel_circ
            prim[1, part, at, :] = pressure
            prim[2, part, at, :] = jnp.abs(vel_circ) + sound
            iv[part, here, :] = (1.0 / ALPHA) / (jnp.abs(vel_ax) + sound)
        pivots, firsts = [], []
        for a in range(rows):
            value = 2.0 + DIAG0 * iv[a, here, :]
            if a:
                value = value - pivots[-1]
            pivots.append(1.0 / value)
            firsts.append(pivots[-1] * firsts[-1] if a else pivots[-1])
        low, high = firsts[-1], pivots[-1]
        for a in reversed(range(rows)):
            if a < rows - 1:
                low = firsts[a] + pivots[a] * low
                high = pivots[a] * high
            piv[a, here, :] = pivots[a]
            phi[a, here, :] = low
            psi[a, here, :] = high
        return carry

    lax.fori_loop(0, chunks, own_tile, 0)

    last = rows - 1

    def chain_copy(side, target):
        return pltpu.make_async_remote_copy(
            src_ref=chain_out.at[side], dst_ref=chain_in.at[side], send_sem=csend.at[side],
            recv_sem=crecv.at[side], device_id=(i, target, c), device_id_type=MESH)

    up_copy = chain_copy(0, jnp.minimum(me + 1, n_ax - 1))
    down_copy = chain_copy(1, jnp.maximum(me - 1, 0))

    def chain_up():
        @pl.when(me == 0)
        def _():
            chain_in[0, 0] = jnp.zeros((width, radial), jnp.float32)
            chain_in[0, 1] = jnp.ones((width, radial), jnp.float32)

        @pl.when(me > 0)
        def _():
            up_copy.wait_recv()

        wall, scale = chain_in[0, 0], chain_in[0, 1]
        den = 1.0 / (1.0 - wall * phi[0])
        mix = phi[last] * wall * den
        following = scale * phi[last] * den
        chain_out[0, 0] = psi[last] + mix * psi[0]
        chain_out[0, 1] = following

        @pl.when(me < n_ax - 1)
        def _():
            up_copy.start()

        inverse = 1.0 / following
        coef[0] = inverse
        coef[1] = mix * inverse

    def chain_down():
        @pl.when(me == n_ax - 1)
        def _():
            chain_in[1, 0] = jnp.zeros((width, radial), jnp.float32)
            chain_in[1, 1] = jnp.ones((width, radial), jnp.float32)

        @pl.when(me < n_ax - 1)
        def _():
            down_copy.wait_recv()

        wall, scale = chain_in[1, 0], chain_in[1, 1]
        den = 1.0 / (1.0 - wall * psi[last])
        mix = psi[0] * wall * den
        following = scale * psi[0] * den
        chain_out[1, 0] = phi[0] + mix * phi[last]
        chain_out[1, 1] = following

        @pl.when(me > 0)
        def _():
            down_copy.start()

        inverse = 1.0 / following
        coef[2] = inverse
        coef[3] = mix * inverse

    lower_half = me < n_ax // 2
    pl.when(lower_half)(chain_up)
    pl.when(jnp.logical_not(lower_half))(chain_down)

    for copy in halos:
        copy.wait_recv()
    sub = lax.broadcasted_iota(jnp.int32, (TILE, radial), 0)
    top = chunks + 1
    for a in range(rows):
        for side, t, edge in ((0, 0, TILE - 1), (1, top, 0)):
            cells = []
            for f in range(fields):
                near = jnp.broadcast_to(halo_in[side, f, pl.ds(a, 1), :], (TILE, radial))
                if f == fields - 1:
                    far = jnp.broadcast_to(halo_in[side, fields, pl.ds(a, 1), :], (TILE, radial))
                    near = jnp.where(sub == edge, near, far)
                cells.append(near)
                pad[f, a, pl.ds(t * TILE, TILE), :] = near
            _, vel_circ, pressure, sound = primitives(cells)
            prim[0, a, pl.ds(t * TILE, TILE), :] = vel_circ
            prim[1, a, pl.ds(t * TILE, TILE), :] = pressure
            prim[2, a, pl.ds(t * TILE, TILE), :] = jnp.abs(vel_circ) + sound

    def behind(low, mid, by):
        return jnp.where(sub < by, pltpu.roll(low, by, 0), pltpu.roll(mid, by, 0))

    def ahead(mid, high):
        return jnp.where(sub == TILE - 1, pltpu.roll(high, TILE - 1, 0), pltpu.roll(mid, TILE - 1, 0))

    def face_tile(j, a, flagged):
        low, mid, high = tile(j), tile(j + 1), tile(jnp.minimum(j + 2, top))
        frac_low, frac_here, frac_high = (pad[fields - 1, a, t, :] for t in (low, mid, high))
        back1 = behind(frac_low, frac_here, 1)
        back2 = behind(frac_low, frac_here, 2)
        following = ahead(frac_here, frac_high)
        frac_left = jnp.where(flagged, sharpen(back2, back1, frac_here, 1.0), back1)
        frac_right = jnp.where(flagged, sharpen(back1, frac_here, following, -1.0), frac_here)
        vel_r, press_r, fast_r = (prim[s, a, mid, :] for s in range(3))
        vel_l, press_l, fast_l = (behind(prim[s, a, low, :], prim[s, a, mid, :], 1) for s in range(3))
        half = 0.5 * jnp.maximum(fast_l, fast_r)
        take_l, take_r = 0.5 * vel_l + half, 0.5 * vel_r - half
        for f in range(fields):
            if f < fields - 1:
                right = pad[f, a, mid, :]
                left = behind(pad[f, a, low, :], right, 1)
            else:
                left, right = frac_left, frac_right
            value = left * take_l + right * take_r
            if f == 3:
                value = value + 0.5 * (press_l + press_r)
            if f == 5:
                value = value + 0.5 * (press_l * vel_l + press_r * vel_r)
            flux[f, a, low, :] = value

    def faces(j, carry):
        for a in range(rows):
            face_tile(j, a, flag_ref[a, tile(j), :] > 0.5)
        return carry

    lax.fori_loop(0, chunks, faces, 0)
    for a in range(rows):
        face_tile(chunks, a, jnp.broadcast_to(halo_in[1, fields + 1, pl.ds(a, 1), :], (TILE, radial)) > 0.5)

    def right_side(j, carry):
        for a in range(rows):
            scale = iv[a, tile(j), :]
            for f in range(fields):
                here = flux[f, a, tile(j), :]
                change = ahead(here, flux[f, a, tile(j + 1), :]) - here
                bg[f, a, tile(j), :] = -scale * (change + weights[0] * pad[f, a, tile(j + 1), :])
        return carry

    lax.fori_loop(0, chunks, right_side, 0)

    pl.when(lower_half)(chain_down)
    pl.when(jnp.logical_not(lower_half))(chain_up)

    wall_l, wall_u = chain_in[0, 0], chain_in[1, 0]
    keep_l, keep_u = 1.0 - wall_l * phi[0], 1.0 - wall_u * psi[last]
    cross_l, cross_u = wall_l * phi[last], wall_u * psi[0]
    inv_det = 1.0 / (keep_l * keep_u - cross_l * cross_u)
    coef[4] = wall_l * keep_u * inv_det
    coef[5] = wall_l * cross_u * inv_det
    coef[6] = wall_u * cross_l * inv_det
    coef[7] = wall_u * keep_l * inv_det

    def span(ref, *index):
        return ref.at[index]

    def zcopy(j, step):
        dest = lax.rem(base + lax.rem(j, 2) + 2 * step, n_ax)
        slot = lax.rem(me - dest + n_ax, n_ax)
        pick = jnp.where(me < dest, 0, 1)
        return pltpu.make_async_remote_copy(
            src_ref=ps.at[pick, :, tile(j), :], dst_ref=zrecv.at[slot, :, tile(j), :],
            send_sem=zsend.at[j], recv_sem=zrecv_sem.at[j],
            device_id=(i, dest, c), device_id_type=MESH)

    def forward_copy(j):
        return pltpu.make_async_remote_copy(
            src_ref=ag_out.at[:, :, tile(j), :], dst_ref=ag_in.at[:, :, tile(j), :],
            send_sem=fsend.at[j], recv_sem=frecv.at[j],
            device_id=(i, sibling, c), device_id_type=MESH)

    def out_copy(j):
        return pltpu.make_async_copy(bg.at[:, :, tile(j), :], out_hbm.at[0, :, :, tile(j), :], osem.at[j])

    def reduce_chunk(j):
        at = tile(j)
        for k in range(1, n_inst):
            ycopy(k, j).wait_recv()

        def one_field(f, carry):
            running = None
            values = []
            for a in range(rows):
                other = weights[1] * rem[0, f, a, at, :]
                for k in range(2, n_inst):
                    other = other + weights[k] * rem[k - 1, f, a, at, :]
                value = bg[f, a, at, :] - iv[a, at, :] * other
                running = piv[a, at, :] * (value if a == 0 else value + running)
                values.append(running)
            solved = values[-1]
            bg[f, last, at, :] = solved
            for a in reversed(range(last)):
                solved = values[a] + piv[a, at, :] * solved
                bg[f, a, at, :] = solved
            ps[0, f, at, :] = coef[0, at, :] * values[-1] + coef[1, at, :] * solved
            ps[1, f, at, :] = coef[2, at, :] * solved + coef[3, at, :] * values[-1]
            return carry

        lax.fori_loop(0, fields, one_field, 0)

        @pl.when(core != lax.rem(j, 2))
        def _():
            zcopy(j, 0).start()

        for step in range(1, n_ax // 2):
            zcopy(j, step).start()

    def gather_chunk(j):
        at = tile(j)

        @pl.when(core == lax.rem(j, 2))
        def _():
            landed = zrecv.at[pl.ds(1, n_ax - 1), :, at, :]
            pltpu.make_async_copy(landed, landed, zrecv_sem.at[j]).wait()

            def one_field(f, carry):
                down = jnp.zeros((TILE, radial), jnp.float32)
                up = jnp.zeros((TILE, radial), jnp.float32)
                for slot in range(1, n_ax):
                    source = lax.rem(me + slot, n_ax)
                    value = zrecv[slot, f, at, :]
                    down = down + jnp.where(source < base, value, 0.0)
                    up = up + jnp.where(source > base + 1, value, 0.0)
                beside = jnp.where(core == 0, zrecv[1, f, at, :], zrecv[n_ax - 1, f, at, :])
                ag_out[0, f, at, :] = down + jnp.where(core == 0, ps[0, f, at, :], 0.0)
                ag_out[1, f, at, :] = up + jnp.where(core == 0, 0.0, ps[1, f, at, :])
                ag_in[0, f, at, :] = down + jnp.where(core == 0, 0.0, beside)
                ag_in[1, f, at, :] = up + jnp.where(core == 0, beside, 0.0)
                return carry

            lax.fori_loop(0, fields, one_field, 0)
            forward_copy(j).start()

    def finish_chunk(j):
        at = tile(j)

        @pl.when(core != lax.rem(j, 2))
        def _():
            forward_copy(j).wait_recv()

        def one_field(f, carry):
            low = chain_in[0, 1, at, :] * ag_in[0, f, at, :]
            high = chain_in[1, 1, at, :] * ag_in[1, f, at, :]
            first = bg[f, 0, at, :] + low * phi[0, at, :] + high * psi[0, at, :]
            final = bg[f, last, at, :] + low * phi[last, at, :] + high * psi[last, at, :]
            low = low + coef[4, at, :] * first + coef[5, at, :] * final
            high = high + coef[6, at, :] * first + coef[7, at, :] * final
            for a in range(rows):
                delta = bg[f, a, at, :] + low * phi[a, at, :] + high * psi[a, at, :]
                bg[f, a, at, :] = pad[f, a, tile(j + 1), :] + delta
            return carry

        lax.fori_loop(0, fields, one_field, 0)
        out_copy(j).start()

    def step(j, carry):
        @pl.when(j < chunks)
        def _():
            reduce_chunk(j)

        @pl.when(jnp.logical_and(j >= 1, j <= chunks))
        def _():
            gather_chunk(j - 1)

        @pl.when(j >= 2)
        def _():
            finish_chunk(j - 2)

        return carry

    lax.fori_loop(0, chunks + 2, step, 0)

    for copy in halos:
        copy.wait_send()

    @pl.when(me < n_ax - 1)
    def _():
        up_copy.wait_send()

    @pl.when(me > 0)
    def _():
        down_copy.wait_send()

    def drain(j, carry):
        for k in range(1, n_inst):
            ycopy(k, j).wait_send()

        @pl.when(core != lax.rem(j, 2))
        def _():
            zcopy(j, 0).wait_send()

        for s in range(1, n_ax // 2):
            zcopy(j, s).wait_send()

        @pl.when(core == lax.rem(j, 2))
        def _():
            forward_copy(j).wait_send()

        out_copy(j).wait()
        return carry

    lax.fori_loop(0, chunks, drain, 0)


def local(mesh_shape, flow_state, thinc_flags):
    n_inst, n_ax, n_circ = mesh_shape["inst"], mesh_shape["ax"], mesh_shape["circ"]
    _, fields, rows, width, radial = flow_state.shape
    chunks = width // TILE
    flags = jnp.broadcast_to(thinc_flags[0].astype(jnp.float32)[:, :, None], (rows, width, radial))
    f32 = jnp.float32
    scratch = [
        pltpu.VMEM((fields, rows, width + 2 * TILE, radial), f32),
        pltpu.VMEM((3, rows, width + 2 * TILE, radial), f32),
        pltpu.VMEM((fields, rows, width + TILE, radial), f32),
        pltpu.VMEM((fields, rows, width, radial), f32),
        pltpu.VMEM((rows, width, radial), f32),
        pltpu.VMEM((rows, width, radial), f32),
        pltpu.VMEM((rows, width, radial), f32),
        pltpu.VMEM((rows, width, radial), f32),
        pltpu.VMEM((n_inst - 1, fields, rows, width, radial), f32),
        pltpu.VMEM((2, fields + 2, rows, radial), f32),
        pltpu.VMEM((2, fields + 2, rows, radial), f32),
        pltpu.VMEM((2, 2, width, radial), f32),
        pltpu.VMEM((2, 2, width, radial), f32),
        pltpu.VMEM((8, width, radial), f32),
        pltpu.VMEM((2, fields, width, radial), f32),
        pltpu.VMEM((n_ax, fields, width, radial), f32),
        pltpu.VMEM((2, fields, width, radial), f32),
        pltpu.VMEM((2, fields, width, radial), f32),
        pltpu.SemaphoreType.DMA,
        pltpu.SemaphoreType.DMA((n_inst - 1, chunks)),
        pltpu.SemaphoreType.DMA((n_inst - 1, chunks)),
        pltpu.SemaphoreType.DMA((2,)),
        pltpu.SemaphoreType.DMA((2,)),
        pltpu.SemaphoreType.DMA((2,)),
        pltpu.SemaphoreType.DMA((2,)),
        pltpu.SemaphoreType.DMA((chunks,)),
        pltpu.SemaphoreType.DMA((chunks,)),
        pltpu.SemaphoreType.DMA((chunks,)),
        pltpu.SemaphoreType.DMA((chunks,)),
        pltpu.SemaphoreType.DMA((chunks,)),
    ]
    return pl.pallas_call(
        functools.partial(
            kernel, (n_inst, n_ax, n_circ, rows, width, radial), spectral_weights(n_inst)
        ),
        out_shape=jax.ShapeDtypeStruct(flow_state.shape, f32),
        in_specs=[pl.BlockSpec(memory_space=pl.ANY), pl.BlockSpec(memory_space=pltpu.VMEM)],
        out_specs=pl.BlockSpec(memory_space=pl.ANY),
        scratch_shapes=scratch,
        compiler_params=pltpu.CompilerParams(
            collective_id=0, has_side_effects=True, vmem_limit_bytes=48 * 1024 * 1024
        ),
    )(flow_state, flags)


def solution(mesh):
    return jax.shard_map(
        functools.partial(local, dict(mesh.shape)),
        mesh=mesh,
        in_specs=(P("inst", None, "ax", "circ", None), P("inst", "ax", "circ")),
        out_specs=P("inst", None, "ax", "circ", None),
        check_vma=False,
    )
```

```python
import functools
import math

import jax
import jax.numpy as jnp
import numpy as np
from jax import lax
from jax.experimental import pallas as pl
from jax.experimental.pallas import tpu as pltpu
from jax.sharding import PartitionSpec as P

G_LIQ = 4.4
P_LIQ = 6.0
G_GAS = 1.4
BETA = 1.6
EPSA = 0.1
ALPHA = 4.0
DIAG0 = 0.016
OMEGA = 1.0
NU_T = 0.25
MESH = pl.DeviceIdType.MESH
TILE = 8
PIECES = ((0, 4), (4, 2), (6, 1))


def spectral_weights(count):
    weights = []
    for k in range(count):
        if k == 0:
            first, second = 0.0, -(count * count + 2) / 12.0
        else:
            angle = math.pi * k / count
            parity = 1.0 if k % 2 == 0 else -1.0
            first = 0.5 * parity * math.cos(angle) / math.sin(angle)
            second = -parity / (2.0 * math.sin(angle) ** 2)
        weights.append(float(np.float32(OMEGA * first - NU_T * OMEGA * OMEGA * second)))
    return weights


def sharpen(lower_val, centre, upper_val, offset):
    average = 0.5 * (lower_val + upper_val)
    difference = upper_val - lower_val
    steepness = 2.0 * (centre - average) / (jnp.abs(difference) + EPSA)
    return average + 0.5 * difference * jnp.tanh(BETA * (steepness + offset))


def primitives(q):
    density = q[0] + q[1]
    inv = 1.0 / density
    vel_ax = q[2] * inv
    vel_circ = q[3] * inv
    vel_rad = q[4] * inv
    fraction = q[6]
    gamma_term = fraction / (G_LIQ - 1.0) + (1.0 - fraction) / (G_GAS - 1.0)
    stiff_term = fraction * (G_LIQ * P_LIQ / (G_LIQ - 1.0))
    kinetic = 0.5 * (vel_ax * q[2] + vel_circ * q[3] + vel_rad * q[4])
    inv_gamma = 1.0 / gamma_term
    pressure = (q[5] - kinetic - stiff_term) * inv_gamma
    sound = jnp.sqrt((pressure + (pressure + stiff_term) * inv_gamma) * inv)
    return vel_ax, vel_circ, pressure, sound


def kernel(sizes, weights, q_hbm, flag_ref, out_hbm, pad, prim, flux, bg, iv, piv, phi, psi, rem, flag_wide,
           halo_out, halo_in, chain_out, chain_in, coef, ps, zrecv, ag_out, ag_in,
           load_sem, ysend, yrecv, hsend, hrecv, csend, crecv, zsend, zrecv_sem, fsend, frecv, osem):
    n_inst, n_ax, n_circ, rows, width, radial = sizes
    fields = 7
    chunks = width // TILE
    block = 4 if rows % 4 == 0 else 1
    i, me, c = lax.axis_index("inst"), lax.axis_index("ax"), lax.axis_index("circ")
    core = lax.rem(me, 2)
    base = me - core
    sibling = base + 1 - core
    above, below = lax.rem(c + 1, n_circ), lax.rem(c + n_circ - 1, n_circ)

    def tile(j):
        return pl.ds(pl.multiple_of(j * TILE, TILE), TILE)

    load = pltpu.make_async_copy(q_hbm.at[0], pad.at[:, :, pl.ds(TILE, width), :], load_sem)
    load.start()

    barrier = pltpu.get_barrier_semaphore()
    for k in range(1, n_inst):
        pl.semaphore_signal(barrier, inc=1, device_id=(lax.rem(i + k, n_inst), me, c), device_id_type=MESH)
    for k in range(1, n_ax):
        pl.semaphore_signal(barrier, inc=1, device_id=(i, lax.rem(me + k, n_ax), c), device_id_type=MESH)
    for other in (above, below):
        pl.semaphore_signal(barrier, inc=1, device_id=(i, me, other), device_id_type=MESH)
    pl.semaphore_wait(barrier, n_inst + n_ax)

    units = [(j, 0, fields) for j in range(chunks - 1)]
    units += [(chunks - 1, f0, nf) for f0, nf in PIECES]

    def ycopy(k, u, j, f0, nf):
        return pltpu.make_async_remote_copy(
            src_ref=q_hbm.at[0, pl.ds(f0, nf), :, tile(j), :],
            dst_ref=rem.at[k - 1, pl.ds(f0, nf), :, tile(j), :],
            send_sem=ysend.at[k - 1, u], recv_sem=yrecv.at[k - 1, u],
            device_id=(lax.rem(i + k, n_inst), me, c), device_id_type=MESH)

    for u, (j, f0, nf) in enumerate(units):
        for k in range(1, n_inst):
            ycopy(k, u, j, f0, nf).start()

    flags = flag_ref[0].astype(jnp.float32)
    line = lax.broadcasted_iota(jnp.int32, flags.shape, 0)
    for a in range(rows):
        flag_wide[a] = lax.dot_general(
            jnp.where(line == a, flags, 0.0), jnp.ones((rows, radial), jnp.float32),
            (((0,), (0,)), ((), ())), preferred_element_type=jnp.float32)

    load.wait()

    for f in range(fields):
        halo_out[0, f] = pad[f, :, TILE + width - 1, :]
        halo_out[1, f] = pad[f, :, TILE, :]
    halo_out[0, fields] = pad[fields - 1, :, TILE + width - 2, :]
    halo_out[1, fields] = pad[fields - 1, :, TILE + 1, :]
    first_flags = jnp.broadcast_to(flags[:, 0:1], (rows, radial))
    halo_out[0, fields + 1] = first_flags
    halo_out[1, fields + 1] = first_flags
    halos = [
        pltpu.make_async_remote_copy(
            src_ref=halo_out.at[side], dst_ref=halo_in.at[side], send_sem=hsend.at[side],
            recv_sem=hrecv.at[side], device_id=(i, me, (above, below)[side]), device_id_type=MESH)
        for side in range(2)
    ]
    for copy in halos:
        copy.start()

    def own_tile(j, carry):
        at = tile(j + 1)
        here = tile(j)
        for a0 in range(0, rows, block):
            part = pl.ds(a0, block)
            vel_ax, vel_circ, pressure, sound = primitives([pad[f, part, at, :] for f in range(fields)])
            prim[0, part, at, :] = vel_circ
            prim[1, part, at, :] = pressure
            prim[2, part, at, :] = jnp.abs(vel_circ) + sound
            iv[part, here, :] = (1.0 / ALPHA) / (jnp.abs(vel_ax) + sound)
        pivots, firsts = [], []
        for a in range(rows):
            value = 2.0 + DIAG0 * iv[a, here, :]
            if a:
                value = value - pivots[-1]
            pivots.append(1.0 / value)
            firsts.append(pivots[-1] * firsts[-1] if a else pivots[-1])
        low, high = firsts[-1], pivots[-1]
        for a in reversed(range(rows)):
            if a < rows - 1:
                low = firsts[a] + pivots[a] * low
                high = pivots[a] * high
            piv[a, here, :] = pivots[a]
            phi[a, here, :] = low
            psi[a, here, :] = high
        return carry

    lax.fori_loop(0, chunks, own_tile, 0)

    last = rows - 1

    def chain_copy(side, target):
        return pltpu.make_async_remote_copy(
            src_ref=chain_out.at[side], dst_ref=chain_in.at[side], send_sem=csend.at[side],
            recv_sem=crecv.at[side], device_id=(i, target, c), device_id_type=MESH)

    up_copy = chain_copy(0, jnp.minimum(me + 1, n_ax - 1))
    down_copy = chain_copy(1, jnp.maximum(me - 1, 0))

    def chain_up():
        @pl.when(me == 0)
        def _():
            chain_in[0, 0] = jnp.zeros((width, radial), jnp.float32)
            chain_in[0, 1] = jnp.ones((width, radial), jnp.float32)

        @pl.when(me > 0)
        def _():
            up_copy.wait_recv()

        wall, scale = chain_in[0, 0], chain_in[0, 1]
        den = 1.0 / (1.0 - wall * phi[0])
        mix = phi[last] * wall * den
        following = scale * phi[last] * den
        chain_out[0, 0] = psi[last] + mix * psi[0]
        chain_out[0, 1] = following

        @pl.when(me < n_ax - 1)
        def _():
            up_copy.start()

        inverse = 1.0 / following
        coef[0] = inverse
        coef[1] = mix * inverse

    def chain_down():
        @pl.when(me == n_ax - 1)
        def _():
            chain_in[1, 0] = jnp.zeros((width, radial), jnp.float32)
            chain_in[1, 1] = jnp.ones((width, radial), jnp.float32)

        @pl.when(me < n_ax - 1)
        def _():
            down_copy.wait_recv()

        wall, scale = chain_in[1, 0], chain_in[1, 1]
        den = 1.0 / (1.0 - wall * psi[last])
        mix = psi[0] * wall * den
        following = scale * psi[0] * den
        chain_out[1, 0] = phi[0] + mix * phi[last]
        chain_out[1, 1] = following

        @pl.when(me > 0)
        def _():
            down_copy.start()

        inverse = 1.0 / following
        coef[2] = inverse
        coef[3] = mix * inverse

    lower_half = me < n_ax // 2
    pl.when(lower_half)(chain_up)
    pl.when(jnp.logical_not(lower_half))(chain_down)

    for copy in halos:
        copy.wait_recv()
    sub = lax.broadcasted_iota(jnp.int32, (TILE, radial), 0)
    top = chunks + 1
    for a in range(rows):
        for side, t, edge in ((0, 0, TILE - 1), (1, top, 0)):
            cells = []
            for f in range(fields):
                near = jnp.broadcast_to(halo_in[side, f, pl.ds(a, 1), :], (TILE, radial))
                if f == fields - 1:
                    far = jnp.broadcast_to(halo_in[side, fields, pl.ds(a, 1), :], (TILE, radial))
                    near = jnp.where(sub == edge, near, far)
                cells.append(near)
                pad[f, a, pl.ds(t * TILE, TILE), :] = near
            _, vel_circ, pressure, sound = primitives(cells)
            prim[0, a, pl.ds(t * TILE, TILE), :] = vel_circ
            prim[1, a, pl.ds(t * TILE, TILE), :] = pressure
            prim[2, a, pl.ds(t * TILE, TILE), :] = jnp.abs(vel_circ) + sound

    def behind(low, mid, by):
        return jnp.where(sub < by, pltpu.roll(low, by, 0), pltpu.roll(mid, by, 0))

    def ahead(mid, high):
        return jnp.where(sub == TILE - 1, pltpu.roll(high, TILE - 1, 0), pltpu.roll(mid, TILE - 1, 0))

    def face_tile(j, a, flagged):
        low, mid, high = tile(j), tile(j + 1), tile(jnp.minimum(j + 2, top))
        frac_low, frac_here, frac_high = (pad[fields - 1, a, t, :] for t in (low, mid, high))
        back1 = behind(frac_low, frac_here, 1)
        back2 = behind(frac_low, frac_here, 2)
        following = ahead(frac_here, frac_high)
        frac_left = jnp.where(flagged, sharpen(back2, back1, frac_here, 1.0), back1)
        frac_right = jnp.where(flagged, sharpen(back1, frac_here, following, -1.0), frac_here)
        vel_r, press_r, fast_r = (prim[s, a, mid, :] for s in range(3))
        vel_l, press_l, fast_l = (behind(prim[s, a, low, :], prim[s, a, mid, :], 1) for s in range(3))
        half = 0.5 * jnp.maximum(fast_l, fast_r)
        take_l, take_r = 0.5 * vel_l + half, 0.5 * vel_r - half
        for f in range(fields):
            if f < fields - 1:
                right = pad[f, a, mid, :]
                left = behind(pad[f, a, low, :], right, 1)
            else:
                left, right = frac_left, frac_right
            value = left * take_l + right * take_r
            if f == 3:
                value = value + 0.5 * (press_l + press_r)
            if f == 5:
                value = value + 0.5 * (press_l * vel_l + press_r * vel_r)
            flux[f, a, low, :] = value

    def faces(j, carry):
        for a in range(rows):
            face_tile(j, a, flag_wide[a, tile(j), :] > 0.5)
        return carry

    lax.fori_loop(0, chunks, faces, 0)
    for a in range(rows):
        face_tile(chunks, a, jnp.broadcast_to(halo_in[1, fields + 1, pl.ds(a, 1), :], (TILE, radial)) > 0.5)

    def right_side(j, carry):
        for a in range(rows):
            scale = iv[a, tile(j), :]
            for f in range(fields):
                here = flux[f, a, tile(j), :]
                change = ahead(here, flux[f, a, tile(j + 1), :]) - here
                bg[f, a, tile(j), :] = -scale * (change + weights[0] * pad[f, a, tile(j + 1), :])
        return carry

    lax.fori_loop(0, chunks, right_side, 0)

    pl.when(lower_half)(chain_down)
    pl.when(jnp.logical_not(lower_half))(chain_up)

    wall_l, wall_u = chain_in[0, 0], chain_in[1, 0]
    keep_l, keep_u = 1.0 - wall_l * phi[0], 1.0 - wall_u * psi[last]
    cross_l, cross_u = wall_l * phi[last], wall_u * psi[0]
    inv_det = 1.0 / (keep_l * keep_u - cross_l * cross_u)
    coef[4] = wall_l * keep_u * inv_det
    coef[5] = wall_l * cross_u * inv_det
    coef[6] = wall_u * cross_l * inv_det
    coef[7] = wall_u * keep_l * inv_det

    def zcopy(dest, u, j, f0, nf):
        slot = lax.rem(me - dest + n_ax, n_ax)
        pick = jnp.where(me < dest, 0, 1)
        return pltpu.make_async_remote_copy(
            src_ref=ps.at[pick, pl.ds(f0, nf), tile(j), :],
            dst_ref=zrecv.at[slot, pl.ds(f0, nf), tile(j), :],
            send_sem=zsend.at[u], recv_sem=zrecv_sem.at[u],
            device_id=(i, dest, c), device_id_type=MESH)

    def each_target(unit, direct, act):
        if direct:
            for step in range(1, n_ax):
                act(zcopy(lax.rem(me + step, n_ax), *unit))
            return
        first = base + lax.rem(unit[0], 2)

        @pl.when(first != me)
        def _():
            act(zcopy(first, *unit))

        for step in range(1, n_ax // 2):
            act(zcopy(lax.rem(first + 2 * step, n_ax), *unit))

    def forward_copy(j):
        return pltpu.make_async_remote_copy(
            src_ref=ag_out.at[:, :, tile(j), :], dst_ref=ag_in.at[:, :, tile(j), :],
            send_sem=fsend.at[j], recv_sem=frecv.at[j],
            device_id=(i, sibling, c), device_id_type=MESH)

    def out_copy(u, j, f0, nf):
        return pltpu.make_async_copy(
            bg.at[pl.ds(f0, nf), :, tile(j), :], out_hbm.at[0, pl.ds(f0, nf), :, tile(j), :], osem.at[u])

    def each_field(unit, act):
        def body(f, carry):
            act(f)
            return carry

        lax.fori_loop(unit[2], unit[2] + unit[3], body, 0)

    def reduce_unit(unit, direct):
        at = tile(unit[1])
        for k in range(1, n_inst):
            ycopy(k, *unit).wait_recv()

        def one_field(f):
            running = None
            values = []
            for a in range(rows):
                other = weights[1] * rem[0, f, a, at, :]
                for k in range(2, n_inst):
                    other = other + weights[k] * rem[k - 1, f, a, at, :]
                value = bg[f, a, at, :] - iv[a, at, :] * other
                running = piv[a, at, :] * (value if a == 0 else value + running)
                values.append(running)
            solved = values[-1]
            bg[f, last, at, :] = solved
            for a in reversed(range(last)):
                solved = values[a] + piv[a, at, :] * solved
                bg[f, a, at, :] = solved
            ps[0, f, at, :] = coef[0, at, :] * values[-1] + coef[1, at, :] * solved
            ps[1, f, at, :] = coef[2, at, :] * solved + coef[3, at, :] * values[-1]

        each_field(unit, one_field)
        each_target(unit, direct, lambda copy: copy.start())

    def landed(unit):
        block = zrecv.at[pl.ds(1, n_ax - 1), pl.ds(unit[2], unit[3]), tile(unit[1]), :]
        pltpu.make_async_copy(block, block, zrecv_sem.at[unit[0]]).wait()

    def sums(f, at, lower, upper):
        down = jnp.zeros((TILE, radial), jnp.float32)
        up = jnp.zeros((TILE, radial), jnp.float32)
        for slot in range(1, n_ax):
            source = lax.rem(me + slot, n_ax)
            value = zrecv[slot, f, at, :]
            down = down + jnp.where(source < lower, value, 0.0)
            up = up + jnp.where(source > upper, value, 0.0)
        return down, up

    def gather_unit(unit):
        at = tile(unit[1])

        @pl.when(core == lax.rem(unit[0], 2))
        def _():
            landed(unit)

            def one_field(f):
                down, up = sums(f, at, base, base + 1)
                beside = jnp.where(core == 0, zrecv[1, f, at, :], zrecv[n_ax - 1, f, at, :])
                ag_out[0, f, at, :] = down + jnp.where(core == 0, ps[0, f, at, :], 0.0)
                ag_out[1, f, at, :] = up + jnp.where(core == 0, 0.0, ps[1, f, at, :])
                ag_in[0, f, at, :] = down + jnp.where(core == 0, 0.0, beside)
                ag_in[1, f, at, :] = up + jnp.where(core == 0, beside, 0.0)

            each_field(unit, one_field)
            forward_copy(unit[0]).start()

    def finish_unit(unit, direct):
        at = tile(unit[1])
        if direct:
            landed(unit)
        else:
            @pl.when(core != lax.rem(unit[0], 2))
            def _():
                forward_copy(unit[0]).wait_recv()

        def one_field(f):
            low, high = sums(f, at, me, me) if direct else (ag_in[0, f, at, :], ag_in[1, f, at, :])
            low = chain_in[0, 1, at, :] * low
            high = chain_in[1, 1, at, :] * high
            first = bg[f, 0, at, :] + low * phi[0, at, :] + high * psi[0, at, :]
            final = bg[f, last, at, :] + low * phi[last, at, :] + high * psi[last, at, :]
            low = low + coef[4, at, :] * first + coef[5, at, :] * final
            high = high + coef[6, at, :] * first + coef[7, at, :] * final
            for a in range(rows):
                delta = bg[f, a, at, :] + low * phi[a, at, :] + high * psi[a, at, :]
                bg[f, a, at, :] = pad[f, a, tile(unit[1] + 1), :] + delta

        each_field(unit, one_field)
        out_copy(*unit).start()

    whole = chunks - 1
    pieces = [(u, *units[u]) for u in range(whole, len(units))]

    def entire(j):
        return (j, j, 0, fields)

    def step(j, carry):
        reduce_unit(entire(j), False)

        @pl.when(j >= 1)
        def _():
            gather_unit(entire(j - 1))

        @pl.when(j >= 2)
        def _():
            finish_unit(entire(j - 2), False)

        return carry

    lax.fori_loop(0, whole, step, 0)
    tasks = []
    if whole >= 2:
        tasks.append(lambda: finish_unit(entire(whole - 2), False))
    if whole >= 1:
        tasks.insert(0, lambda: gather_unit(entire(whole - 1)))
        tasks.append(lambda: finish_unit(entire(whole - 1), False))
    if tasks:
        tasks.pop(0)()
    for piece in pieces:
        reduce_unit(piece, True)
        if tasks:
            tasks.pop(0)()
    for task in tasks:
        task()
    for piece in pieces:
        finish_unit(piece, True)

    for copy in halos:
        copy.wait_send()

    @pl.when(me < n_ax - 1)
    def _():
        up_copy.wait_send()

    @pl.when(me > 0)
    def _():
        down_copy.wait_send()

    def settle(unit, direct):
        for k in range(1, n_inst):
            ycopy(k, *unit).wait_send()
        each_target(unit, direct, lambda copy: copy.wait_send())
        if not direct:
            @pl.when(core == lax.rem(unit[0], 2))
            def _():
                forward_copy(unit[0]).wait_send()
        out_copy(*unit).wait()

    def drain(j, carry):
        settle(entire(j), False)
        return carry

    lax.fori_loop(0, whole, drain, 0)
    for piece in pieces:
        settle(piece, True)


def local(mesh_shape, flow_state, thinc_flags):
    n_inst, n_ax, n_circ = mesh_shape["inst"], mesh_shape["ax"], mesh_shape["circ"]
    _, fields, rows, width, radial = flow_state.shape
    chunks = width // TILE
    n_units = chunks - 1 + len(PIECES)
    f32 = jnp.float32
    scratch = [
        pltpu.VMEM((fields, rows, width + 2 * TILE, radial), f32),
        pltpu.VMEM((3, rows, width + 2 * TILE, radial), f32),
        pltpu.VMEM((fields, rows, width + TILE, radial), f32),
        pltpu.VMEM((fields, rows, width, radial), f32),
        pltpu.VMEM((rows, width, radial), f32),
        pltpu.VMEM((rows, width, radial), f32),
        pltpu.VMEM((rows, width, radial), f32),
        pltpu.VMEM((rows, width, radial), f32),
        pltpu.VMEM((n_inst - 1, fields, rows, width, radial), f32),
        pltpu.VMEM((rows, width, radial), f32),
        pltpu.VMEM((2, fields + 2, rows, radial), f32),
        pltpu.VMEM((2, fields + 2, rows, radial), f32),
        pltpu.VMEM((2, 2, width, radial), f32),
        pltpu.VMEM((2, 2, width, radial), f32),
        pltpu.VMEM((8, width, radial), f32),
        pltpu.VMEM((2, fields, width, radial), f32),
        pltpu.VMEM((n_ax, fields, width, radial), f32),
        pltpu.VMEM((2, fields, width, radial), f32),
        pltpu.VMEM((2, fields, width, radial), f32),
        pltpu.SemaphoreType.DMA,
        pltpu.SemaphoreType.DMA((n_inst - 1, n_units)),
        pltpu.SemaphoreType.DMA((n_inst - 1, n_units)),
        pltpu.SemaphoreType.DMA((2,)),
        pltpu.SemaphoreType.DMA((2,)),
        pltpu.SemaphoreType.DMA((2,)),
        pltpu.SemaphoreType.DMA((2,)),
        pltpu.SemaphoreType.DMA((n_units,)),
        pltpu.SemaphoreType.DMA((n_units,)),
        pltpu.SemaphoreType.DMA((n_units,)),
        pltpu.SemaphoreType.DMA((n_units,)),
        pltpu.SemaphoreType.DMA((n_units,)),
    ]
    return pl.pallas_call(
        functools.partial(
            kernel, (n_inst, n_ax, n_circ, rows, width, radial), spectral_weights(n_inst)
        ),
        out_shape=jax.ShapeDtypeStruct(flow_state.shape, f32),
        in_specs=[pl.BlockSpec(memory_space=pl.ANY), pl.BlockSpec(memory_space=pltpu.VMEM)],
        out_specs=pl.BlockSpec(memory_space=pl.ANY),
        scratch_shapes=scratch,
        compiler_params=pltpu.CompilerParams(
            collective_id=0, has_side_effects=True, vmem_limit_bytes=60 * 1024 * 1024
        ),
    )(flow_state, thinc_flags)


def solution(mesh):
    return jax.shard_map(
        functools.partial(local, dict(mesh.shape)),
        mesh=mesh,
        in_specs=(P("inst", None, "ax", "circ", None), P("inst", "ax", "circ")),
        out_specs=P("inst", None, "ax", "circ", None),
        check_vma=False,
    )
```

```python
import functools
import math

import jax
import jax.numpy as jnp
import numpy as np
from jax import lax
from jax.experimental import pallas as pl
from jax.experimental.pallas import tpu as pltpu
from jax.sharding import PartitionSpec as P

G_LIQ = 4.4
P_LIQ = 6.0
G_GAS = 1.4
BETA = 1.6
EPSA = 0.1
ALPHA = 4.0
DIAG0 = 0.016
OMEGA = 1.0
NU_T = 0.25
MESH = pl.DeviceIdType.MESH
TILE = 8
PIECES = ((0, 4), (4, 2), (6, 1))


def spectral_weights(count):
    weights = []
    for k in range(count):
        if k == 0:
            first, second = 0.0, -(count * count + 2) / 12.0
        else:
            angle = math.pi * k / count
            parity = 1.0 if k % 2 == 0 else -1.0
            first = 0.5 * parity * math.cos(angle) / math.sin(angle)
            second = -parity / (2.0 * math.sin(angle) ** 2)
        weights.append(float(np.float32(OMEGA * first - NU_T * OMEGA * OMEGA * second)))
    return weights


def sharpen(lower_val, centre, upper_val, offset):
    average = 0.5 * (lower_val + upper_val)
    difference = upper_val - lower_val
    steepness = 2.0 * (centre - average) / (jnp.abs(difference) + EPSA)
    return average + 0.5 * difference * jnp.tanh(BETA * (steepness + offset))


def primitives(q):
    density = q[0] + q[1]
    inv = 1.0 / density
    vel_ax = q[2] * inv
    vel_circ = q[3] * inv
    vel_rad = q[4] * inv
    fraction = q[6]
    gamma_term = fraction / (G_LIQ - 1.0) + (1.0 - fraction) / (G_GAS - 1.0)
    stiff_term = fraction * (G_LIQ * P_LIQ / (G_LIQ - 1.0))
    kinetic = 0.5 * (vel_ax * q[2] + vel_circ * q[3] + vel_rad * q[4])
    inv_gamma = 1.0 / gamma_term
    pressure = (q[5] - kinetic - stiff_term) * inv_gamma
    sound = jnp.sqrt((pressure + (pressure + stiff_term) * inv_gamma) * inv)
    return vel_ax, vel_circ, pressure, sound


def kernel(sizes, weights, q_hbm, flag_ref, out_hbm, pad, prim, flux, bg, iv, piv, phi, psi, rem, flag_wide,
           halo_out, halo_in, line_out, line_in, back_out, chain_in, coef, ps, zrecv, ag_out, ag_in,
           load_sem, ysend, yrecv, hsend, hrecv, csend, crecv, bsend, brecv, zsend, zrecv_sem, fsend, frecv, osem):
    n_inst, n_ax, n_circ, rows, width, radial = sizes
    fields = 7
    chunks = width // TILE
    block = 4 if rows % 4 == 0 else 1
    i, me, c = lax.axis_index("inst"), lax.axis_index("ax"), lax.axis_index("circ")
    core = lax.rem(me, 2)
    base = me - core
    sibling = base + 1 - core
    above, below = lax.rem(c + 1, n_circ), lax.rem(c + n_circ - 1, n_circ)

    def tile(j):
        return pl.ds(pl.multiple_of(j * TILE, TILE), TILE)

    load = pltpu.make_async_copy(q_hbm.at[0], pad.at[:, :, pl.ds(TILE, width), :], load_sem)
    load.start()

    barrier = pltpu.get_barrier_semaphore()
    for k in range(1, n_inst):
        pl.semaphore_signal(barrier, inc=1, device_id=(lax.rem(i + k, n_inst), me, c), device_id_type=MESH)
    for k in range(1, n_ax):
        pl.semaphore_signal(barrier, inc=1, device_id=(i, lax.rem(me + k, n_ax), c), device_id_type=MESH)
    for other in (above, below):
        pl.semaphore_signal(barrier, inc=1, device_id=(i, me, other), device_id_type=MESH)
    pl.semaphore_wait(barrier, n_inst + n_ax)

    units = [(j, 0, fields) for j in range(chunks - 1)]
    units += [(chunks - 1, f0, nf) for f0, nf in PIECES]

    def ycopy(k, u, j, f0, nf):
        return pltpu.make_async_remote_copy(
            src_ref=q_hbm.at[0, pl.ds(f0, nf), :, tile(j), :],
            dst_ref=rem.at[k - 1, pl.ds(f0, nf), :, tile(j), :],
            send_sem=ysend.at[k - 1, u], recv_sem=yrecv.at[k - 1, u],
            device_id=(lax.rem(i + k, n_inst), me, c), device_id_type=MESH)

    for u, (j, f0, nf) in enumerate(units):
        for k in range(1, n_inst):
            ycopy(k, u, j, f0, nf).start()

    flags = flag_ref[0].astype(jnp.float32)
    line = lax.broadcasted_iota(jnp.int32, flags.shape, 0)
    for a in range(rows):
        flag_wide[a] = lax.dot_general(
            jnp.where(line == a, flags, 0.0), jnp.ones((rows, radial), jnp.float32),
            (((0,), (0,)), ((), ())), preferred_element_type=jnp.float32)

    load.wait()

    for f in range(fields):
        halo_out[0, f] = pad[f, :, TILE + width - 1, :]
        halo_out[1, f] = pad[f, :, TILE, :]
    halo_out[0, fields] = pad[fields - 1, :, TILE + width - 2, :]
    halo_out[1, fields] = pad[fields - 1, :, TILE + 1, :]
    first_flags = jnp.broadcast_to(flags[:, 0:1], (rows, radial))
    halo_out[0, fields + 1] = first_flags
    halo_out[1, fields + 1] = first_flags
    halos = [
        pltpu.make_async_remote_copy(
            src_ref=halo_out.at[side], dst_ref=halo_in.at[side], send_sem=hsend.at[side],
            recv_sem=hrecv.at[side], device_id=(i, me, (above, below)[side]), device_id_type=MESH)
        for side in range(2)
    ]
    for copy in halos:
        copy.start()

    def own_tile(j, carry):
        at = tile(j + 1)
        here = tile(j)
        for a0 in range(0, rows, block):
            part = pl.ds(a0, block)
            vel_ax, vel_circ, pressure, sound = primitives([pad[f, part, at, :] for f in range(fields)])
            prim[0, part, at, :] = vel_circ
            prim[1, part, at, :] = pressure
            prim[2, part, at, :] = jnp.abs(vel_circ) + sound
            iv[part, here, :] = (1.0 / ALPHA) / (jnp.abs(vel_ax) + sound)
        pivots, firsts = [], []
        for a in range(rows):
            value = 2.0 + DIAG0 * iv[a, here, :]
            if a:
                value = value - pivots[-1]
            pivots.append(1.0 / value)
            firsts.append(pivots[-1] * firsts[-1] if a else pivots[-1])
        low, high = firsts[-1], pivots[-1]
        for a in reversed(range(rows)):
            if a < rows - 1:
                low = firsts[a] + pivots[a] * low
                high = pivots[a] * high
            piv[a, here, :] = pivots[a]
            phi[a, here, :] = low
            psi[a, here, :] = high
        return carry

    lax.fori_loop(0, chunks, own_tile, 0)

    last = rows - 1
    line_out[0] = phi[0]
    line_out[1] = phi[last]
    line_out[2] = psi[last]

    def owner(j):
        return (j * n_ax) // chunks

    def slot_of(device, target):
        return lax.rem(device - target + n_ax, n_ax)

    def line_copy(j):
        return pltpu.make_async_remote_copy(
            src_ref=line_out.at[:, tile(j), :], dst_ref=line_in.at[slot_of(me, owner(j)), :, tile(j), :],
            send_sem=csend.at[j], recv_sem=crecv.at[j],
            device_id=(i, owner(j), c), device_id_type=MESH)

    def back_copy(j, target):
        return pltpu.make_async_remote_copy(
            src_ref=back_out.at[slot_of(target, owner(j)), :, tile(j), :], dst_ref=chain_in.at[:, tile(j), :],
            send_sem=bsend.at[j], recv_sem=brecv.at[j],
            device_id=(i, target, c), device_id_type=MESH)

    def hand_over(j):
        line_in[0, :, tile(j), :] = line_out[:, tile(j), :]

    for j in range(chunks):
        pl.when(me != owner(j))(lambda j=j: line_copy(j).start())
        pl.when(me == owner(j))(lambda j=j: hand_over(j))

    def own_lines(j):
        at = tile(j)
        block_in = line_in.at[pl.ds(1, n_ax - 1), :, at, :]
        pltpu.make_async_copy(block_in, block_in, crecv.at[j]).wait()
        for side in range(2):
            wall = jnp.zeros((TILE, radial), jnp.float32)
            scale = jnp.ones((TILE, radial), jnp.float32)
            for device in range(n_ax) if side == 0 else reversed(range(n_ax)):
                slot = slot_of(device, owner(j))
                back_out[slot, 2 * side, at, :] = wall
                back_out[slot, 2 * side + 1, at, :] = scale
                near, across, far = (line_in[slot, n, at, :] for n in ((0, 1, 2), (2, 1, 0))[side])
                factor = across / (1.0 - wall * near)
                scale = scale * factor
                wall = far + wall * factor * across
        chain_in[:, at, :] = back_out[0, :, at, :]
        for step in range(1, n_ax):
            back_copy(j, lax.rem(me + step, n_ax)).start()

    for copy in halos:
        copy.wait_recv()
    sub = lax.broadcasted_iota(jnp.int32, (TILE, radial), 0)
    top = chunks + 1
    for a in range(rows):
        for side, t, edge in ((0, 0, TILE - 1), (1, top, 0)):
            cells = []
            for f in range(fields):
                near = jnp.broadcast_to(halo_in[side, f, pl.ds(a, 1), :], (TILE, radial))
                if f == fields - 1:
                    far = jnp.broadcast_to(halo_in[side, fields, pl.ds(a, 1), :], (TILE, radial))
                    near = jnp.where(sub == edge, near, far)
                cells.append(near)
                pad[f, a, pl.ds(t * TILE, TILE), :] = near
            _, vel_circ, pressure, sound = primitives(cells)
            prim[0, a, pl.ds(t * TILE, TILE), :] = vel_circ
            prim[1, a, pl.ds(t * TILE, TILE), :] = pressure
            prim[2, a, pl.ds(t * TILE, TILE), :] = jnp.abs(vel_circ) + sound

    for j in range(chunks):
        pl.when(me == owner(j))(lambda j=j: own_lines(j))

    def behind(low, mid, by):
        return jnp.where(sub < by, pltpu.roll(low, by, 0), pltpu.roll(mid, by, 0))

    def ahead(mid, high):
        return jnp.where(sub == TILE - 1, pltpu.roll(high, TILE - 1, 0), pltpu.roll(mid, TILE - 1, 0))

    def face_tile(j, a, flagged):
        low, mid, high = tile(j), tile(j + 1), tile(jnp.minimum(j + 2, top))
        frac_low, frac_here, frac_high = (pad[fields - 1, a, t, :] for t in (low, mid, high))
        back1 = behind(frac_low, frac_here, 1)
        back2 = behind(frac_low, frac_here, 2)
        following = ahead(frac_here, frac_high)
        frac_left = jnp.where(flagged, sharpen(back2, back1, frac_here, 1.0), back1)
        frac_right = jnp.where(flagged, sharpen(back1, frac_here, following, -1.0), frac_here)
        vel_r, press_r, fast_r = (prim[s, a, mid, :] for s in range(3))
        vel_l, press_l, fast_l = (behind(prim[s, a, low, :], prim[s, a, mid, :], 1) for s in range(3))
        half = 0.5 * jnp.maximum(fast_l, fast_r)
        take_l, take_r = 0.5 * vel_l + half, 0.5 * vel_r - half
        for f in range(fields):
            if f < fields - 1:
                right = pad[f, a, mid, :]
                left = behind(pad[f, a, low, :], right, 1)
            else:
                left, right = frac_left, frac_right
            value = left * take_l + right * take_r
            if f == 3:
                value = value + 0.5 * (press_l + press_r)
            if f == 5:
                value = value + 0.5 * (press_l * vel_l + press_r * vel_r)
            flux[f, a, low, :] = value

    def faces(j, carry):
        for a in range(rows):
            face_tile(j, a, flag_wide[a, tile(j), :] > 0.5)
        return carry

    lax.fori_loop(0, chunks, faces, 0)
    for a in range(rows):
        face_tile(chunks, a, jnp.broadcast_to(halo_in[1, fields + 1, pl.ds(a, 1), :], (TILE, radial)) > 0.5)

    def right_side(j, carry):
        for a in range(rows):
            scale = iv[a, tile(j), :]
            for f in range(fields):
                here = flux[f, a, tile(j), :]
                change = ahead(here, flux[f, a, tile(j + 1), :]) - here
                bg[f, a, tile(j), :] = -scale * (change + weights[0] * pad[f, a, tile(j + 1), :])
        return carry

    lax.fori_loop(0, chunks, right_side, 0)

    for j in range(chunks):
        pl.when(me != owner(j))(lambda j=j: back_copy(j, me).wait_recv())

    wall_l, scale_l, wall_u, scale_u = (chain_in[n] for n in range(4))
    for n, wall, scale, near in ((0, wall_l, scale_l, phi[0]), (2, wall_u, scale_u, psi[last])):
        coef[n] = (1.0 - wall * near) / (scale * phi[last])
        coef[n + 1] = wall / scale
    keep_l, keep_u = 1.0 - wall_l * phi[0], 1.0 - wall_u * psi[last]
    cross_l, cross_u = wall_l * phi[last], wall_u * psi[0]
    inv_det = 1.0 / (keep_l * keep_u - cross_l * cross_u)
    coef[4] = wall_l * keep_u * inv_det
    coef[5] = wall_l * cross_u * inv_det
    coef[6] = wall_u * cross_l * inv_det
    coef[7] = wall_u * keep_l * inv_det

    def zcopy(dest, u, j, f0, nf):
        slot = lax.rem(me - dest + n_ax, n_ax)
        pick = jnp.where(me < dest, 0, 1)
        return pltpu.make_async_remote_copy(
            src_ref=ps.at[pick, pl.ds(f0, nf), tile(j), :],
            dst_ref=zrecv.at[slot, pl.ds(f0, nf), tile(j), :],
            send_sem=zsend.at[u], recv_sem=zrecv_sem.at[u],
            device_id=(i, dest, c), device_id_type=MESH)

    def each_target(unit, direct, act):
        if direct:
            for step in range(1, n_ax):
                act(zcopy(lax.rem(me + step, n_ax), *unit))
            return
        first = base + lax.rem(unit[0], 2)

        @pl.when(first != me)
        def _():
            act(zcopy(first, *unit))

        for step in range(1, n_ax // 2):
            act(zcopy(lax.rem(first + 2 * step, n_ax), *unit))

    def forward_copy(j):
        return pltpu.make_async_remote_copy(
            src_ref=ag_out.at[:, :, tile(j), :], dst_ref=ag_in.at[:, :, tile(j), :],
            send_sem=fsend.at[j], recv_sem=frecv.at[j],
            device_id=(i, sibling, c), device_id_type=MESH)

    def out_copy(u, j, f0, nf):
        return pltpu.make_async_copy(
            bg.at[pl.ds(f0, nf), :, tile(j), :], out_hbm.at[0, pl.ds(f0, nf), :, tile(j), :], osem.at[u])

    def each_field(unit, act):
        def body(f, carry):
            act(f)
            return carry

        lax.fori_loop(unit[2], unit[2] + unit[3], body, 0, unroll=True)

    def reduce_unit(unit, direct):
        at = tile(unit[1])
        for k in range(1, n_inst):
            ycopy(k, *unit).wait_recv()

        def one_field(f):
            running = None
            values = []
            for a in range(rows):
                other = weights[1] * rem[0, f, a, at, :]
                for k in range(2, n_inst):
                    other = other + weights[k] * rem[k - 1, f, a, at, :]
                value = bg[f, a, at, :] - iv[a, at, :] * other
                running = piv[a, at, :] * (value if a == 0 else value + running)
                values.append(running)
            solved = values[-1]
            bg[f, last, at, :] = solved
            for a in reversed(range(last)):
                solved = values[a] + piv[a, at, :] * solved
                bg[f, a, at, :] = solved
            ps[0, f, at, :] = coef[0, at, :] * values[-1] + coef[1, at, :] * solved
            ps[1, f, at, :] = coef[2, at, :] * solved + coef[3, at, :] * values[-1]

        each_field(unit, one_field)
        each_target(unit, direct, lambda copy: copy.start())

    def landed(unit):
        block = zrecv.at[pl.ds(1, n_ax - 1), pl.ds(unit[2], unit[3]), tile(unit[1]), :]
        pltpu.make_async_copy(block, block, zrecv_sem.at[unit[0]]).wait()

    def sums(f, at, lower, upper):
        down = jnp.zeros((TILE, radial), jnp.float32)
        up = jnp.zeros((TILE, radial), jnp.float32)
        for slot in range(1, n_ax):
            source = lax.rem(me + slot, n_ax)
            value = zrecv[slot, f, at, :]
            down = down + jnp.where(source < lower, value, 0.0)
            up = up + jnp.where(source > upper, value, 0.0)
        return down, up

    def gather_unit(unit):
        at = tile(unit[1])

        @pl.when(core == lax.rem(unit[0], 2))
        def _():
            landed(unit)

            def one_field(f):
                down, up = sums(f, at, base, base + 1)
                beside = jnp.where(core == 0, zrecv[1, f, at, :], zrecv[n_ax - 1, f, at, :])
                ag_out[0, f, at, :] = down + jnp.where(core == 0, ps[0, f, at, :], 0.0)
                ag_out[1, f, at, :] = up + jnp.where(core == 0, 0.0, ps[1, f, at, :])
                ag_in[0, f, at, :] = down + jnp.where(core == 0, 0.0, beside)
                ag_in[1, f, at, :] = up + jnp.where(core == 0, beside, 0.0)

            each_field(unit, one_field)
            forward_copy(unit[0]).start()

    def finish_unit(unit, direct):
        at = tile(unit[1])
        if direct:
            landed(unit)
        else:
            @pl.when(core != lax.rem(unit[0], 2))
            def _():
                forward_copy(unit[0]).wait_recv()

        def one_field(f):
            low, high = sums(f, at, me, me) if direct else (ag_in[0, f, at, :], ag_in[1, f, at, :])
            low = chain_in[1, at, :] * low
            high = chain_in[3, at, :] * high
            first = bg[f, 0, at, :] + low * phi[0, at, :] + high * psi[0, at, :]
            final = bg[f, last, at, :] + low * phi[last, at, :] + high * psi[last, at, :]
            low = low + coef[4, at, :] * first + coef[5, at, :] * final
            high = high + coef[6, at, :] * first + coef[7, at, :] * final
            for a in range(rows):
                delta = bg[f, a, at, :] + low * phi[a, at, :] + high * psi[a, at, :]
                bg[f, a, at, :] = pad[f, a, tile(unit[1] + 1), :] + delta

        each_field(unit, one_field)
        out_copy(*unit).start()

    whole = chunks - 1
    pieces = [(u, *units[u]) for u in range(whole, len(units))]

    def entire(j):
        return (j, j, 0, fields)

    def step(j, carry):
        @pl.when(j >= 2)
        def _():
            gather_unit(entire(j - 2))

        @pl.when(j >= 3)
        def _():
            finish_unit(entire(j - 3), False)

        reduce_unit(entire(j), False)
        return carry

    lax.fori_loop(0, whole, step, 0)

    def late(act, j, *rest):
        if j >= 0:
            act(entire(j), *rest)

    late(gather_unit, whole - 2)
    late(finish_unit, whole - 3, False)
    for n, piece in enumerate(pieces):
        reduce_unit(piece, True)
        if n == 0:
            late(gather_unit, whole - 1)
            late(finish_unit, whole - 2, False)
        if n == min(1, len(pieces) - 1):
            late(finish_unit, whole - 1, False)
    for piece in pieces:
        finish_unit(piece, True)

    for copy in halos:
        copy.wait_send()

    def settle_lines(j):
        for step in range(1, n_ax):
            back_copy(j, lax.rem(me + step, n_ax)).wait_send()

    for j in range(chunks):
        pl.when(me != owner(j))(lambda j=j: line_copy(j).wait_send())
        pl.when(me == owner(j))(lambda j=j: settle_lines(j))

    def settle(unit, direct):
        for k in range(1, n_inst):
            ycopy(k, *unit).wait_send()
        each_target(unit, direct, lambda copy: copy.wait_send())
        if not direct:
            @pl.when(core == lax.rem(unit[0], 2))
            def _():
                forward_copy(unit[0]).wait_send()
        out_copy(*unit).wait()

    def drain(j, carry):
        settle(entire(j), False)
        return carry

    lax.fori_loop(0, whole, drain, 0)
    for piece in pieces:
        settle(piece, True)


def local(mesh_shape, flow_state, thinc_flags):
    n_inst, n_ax, n_circ = mesh_shape["inst"], mesh_shape["ax"], mesh_shape["circ"]
    _, fields, rows, width, radial = flow_state.shape
    chunks = width // TILE
    n_units = chunks - 1 + len(PIECES)
    f32 = jnp.float32
    scratch = [
        pltpu.VMEM((fields, rows, width + 2 * TILE, radial), f32),
        pltpu.VMEM((3, rows, width + 2 * TILE, radial), f32),
        pltpu.VMEM((fields, rows, width + TILE, radial), f32),
        pltpu.VMEM((fields, rows, width, radial), f32),
        pltpu.VMEM((rows, width, radial), f32),
        pltpu.VMEM((rows, width, radial), f32),
        pltpu.VMEM((rows, width, radial), f32),
        pltpu.VMEM((rows, width, radial), f32),
        pltpu.VMEM((n_inst - 1, fields, rows, width, radial), f32),
        pltpu.VMEM((rows, width, radial), f32),
        pltpu.VMEM((2, fields + 2, rows, radial), f32),
        pltpu.VMEM((2, fields + 2, rows, radial), f32),
        pltpu.VMEM((3, width, radial), f32),
        pltpu.VMEM((n_ax, 3, width, radial), f32),
        pltpu.VMEM((n_ax, 4, width, radial), f32),
        pltpu.VMEM((4, width, radial), f32),
        pltpu.VMEM((8, width, radial), f32),
        pltpu.VMEM((2, fields, width, radial), f32),
        pltpu.VMEM((n_ax, fields, width, radial), f32),
        pltpu.VMEM((2, fields, width, radial), f32),
        pltpu.VMEM((2, fields, width, radial), f32),
        pltpu.SemaphoreType.DMA,
        pltpu.SemaphoreType.DMA((n_inst - 1, n_units)),
        pltpu.SemaphoreType.DMA((n_inst - 1, n_units)),
        pltpu.SemaphoreType.DMA((2,)),
        pltpu.SemaphoreType.DMA((2,)),
        pltpu.SemaphoreType.DMA((chunks,)),
        pltpu.SemaphoreType.DMA((chunks,)),
        pltpu.SemaphoreType.DMA((chunks,)),
        pltpu.SemaphoreType.DMA((chunks,)),
        pltpu.SemaphoreType.DMA((n_units,)),
        pltpu.SemaphoreType.DMA((n_units,)),
        pltpu.SemaphoreType.DMA((n_units,)),
        pltpu.SemaphoreType.DMA((n_units,)),
        pltpu.SemaphoreType.DMA((n_units,)),
    ]
    return pl.pallas_call(
        functools.partial(
            kernel, (n_inst, n_ax, n_circ, rows, width, radial), spectral_weights(n_inst)
        ),
        out_shape=jax.ShapeDtypeStruct(flow_state.shape, f32),
        in_specs=[pl.BlockSpec(memory_space=pl.ANY), pl.BlockSpec(memory_space=pltpu.VMEM)],
        out_specs=pl.BlockSpec(memory_space=pl.ANY),
        scratch_shapes=scratch,
        compiler_params=pltpu.CompilerParams(
            collective_id=0, has_side_effects=True, vmem_limit_bytes=52 * 1024 * 1024
        ),
    )(flow_state, thinc_flags)


def solution(mesh):
    return jax.shard_map(
        functools.partial(local, dict(mesh.shape)),
        mesh=mesh,
        in_specs=(P("inst", None, "ax", "circ", None), P("inst", "ax", "circ")),
        out_specs=P("inst", None, "ax", "circ", None),
        check_vma=False,
    )
```
